32 devices in a mesh: groups: 2 (over y), dp: 16 (over z, x, core).
Axes of the slice: x: 2, y: 2, z: 4, core: 2. Of those that a mesh axis runs over, the one named last changes fastest.
Arguments:
- acts: bfloat16 [4096, 8192], P(('groups', 'dp')), parts along dimension 0, may hold values from -6 to 6
- grad_out: bfloat16 [4096, 1024], P(('groups', 'dp')), parts along dimension 0, may hold values from -6 to 6
- row_adapter: int32 [4096, 1], P(('groups', 'dp')), parts along dimension 0, may hold values from 0 to 63; in each aligned block of 128 rows (0 to 127, 128 to 255, ...) at most 4 rows name the same one
- ranks: int32 [64], replicated, may hold values from 8 to 64
- owner_map: int32 [128], replicated, may hold values from 0 to 127, each once
- down_slots: float32 [256, 32, 8192], P(('groups', 'dp')), parts along dimension 0, may hold values from -0.0625 to 0.0625
- up_slots: float32 [256, 32, 1024], P(('groups', 'dp')), parts along dimension 0, may hold values from -0.1875 to 0.1875
- down_first: float32 [256, 32, 8192], P(('groups', 'dp')), parts along dimension 0, may hold values from -0.0029296875 to 0.0029296875
- down_second: float32 [256, 32, 8192], P(('groups', 'dp')), parts along dimension 0, may hold values from 1e-09 to 1e-07
- up_first: float32 [256, 32, 1024], P(('groups', 'dp')), parts along dimension 0, may hold values from -0.0029296875 to 0.0029296875
- up_second: float32 [256, 32, 1024], P(('groups', 'dp')), parts along dimension 0, may hold values from 1e-09 to 1e-07
Outputs:
- input_grad: bfloat16 [4096, 8192], P(('groups', 'dp')), parts along dimension 0
- new_down: float32 [256, 32, 8192], P(('groups', 'dp')), parts along dimension 0
- new_up: float32 [256, 32, 1024], P(('groups', 'dp')), parts along dimension 0
- new_down_first: float32 [256, 32, 8192], P(('groups', 'dp')), parts along dimension 0
- new_down_second: float32 [256, 32, 8192], P(('groups', 'dp')), parts along dimension 0
- new_up_first: float32 [256, 32, 1024], P(('groups', 'dp')), parts along dimension 0
- new_up_second: float32 [256, 32, 1024], P(('groups', 'dp')), parts along dimension 0
The draws below stay inside these ranges and needn't reach their ends.
There are 2 independent parts, one for each index of `groups`. The reference program is written for one: setup_inputs(seed, part) draws one part's arguments, and reference() takes and returns one part's arrays. A program takes and returns all parts, laid end to end along the dimension named above; an argument that names none is the same for every part. Nothing has to cross between parts.
Inputs may be any that keep to these rules, and one draw needn't show every extreme that they name: `row_adapter`: within the rows of one device no adapter appears on more than 4 rows, and some adapter on exactly 4. `owner_map`: A permutation of the slots; slot s lies on device s // 8 of dp, as entry s % 8 of its share.
All inputs are finite; a program needn't handle non-finite values.
Results may differ from the reference program's by a relative error of at most 0.0067.
Values may be sent and summed in bfloat16 or wider, within the bound.
No kernel may reach another device: no remote copies, remote signals or barrier semaphores. Data moves between devices by JAX's collectives and lax.ppermute only.
A program may use at most 192 MiB of HBM per device.

```python
import math
import jax
import jax.numpy as jnp
import numpy as np
from jax import lax

D = 8192
KV = 1024
R = 64
ADAPTERS = 64
TOK_DEV = 128
HALF = 32
UNITS = 128
CAP = 4
TOKENS = 2048
N_DP = 16


def plant(entries, key, smallest, top_value):
    extent = entries.shape
    spot = [jax.random.randint(jax.random.fold_in(key, axis), (), 0, extent[axis]) for axis in range(len(extent))]
    entries = entries.at[tuple(spot)].set(smallest)
    longest = extent.index(max(extent))
    spot[longest] = (spot[longest] + 1) % extent[longest]
    return entries.at[tuple(spot)].set(top_value)


def block_scale(own_key, extent, cuts, smallest, largest):
    loudness = 1.0
    for dim, blocks in cuts:
        draws = jax.random.uniform(jax.random.fold_in(jax.random.fold_in(own_key, 6), dim), (blocks,), jnp.float32, smallest / len(cuts), largest / len(cuts))
        loudness = loudness * jnp.repeat(jnp.exp(draws), extent[dim] // blocks).reshape((-1,) + (1,) * (len(extent) - 1 - dim))
    return loudness


def shared_out(rng, own, number, rows, number_of, top, limit, lean):
    ranking = jax.random.permutation(rng, number_of)
    heavy_load, usual = portions_of(number_of, rows * top, limit, lean, True), portions_of(number_of, rows * top, limit, lean, False)
    places = jnp.arange(number_of)

    def named(sizes, turn):
        used = int((sizes > 0).sum())
        fixed = max(1, used // 4)
        passed = fixed + (places - fixed + turn * (used - fixed)) % max(1, number_of - fixed)
        return jnp.zeros((number_of,), jnp.int32).at[ranking[jnp.where(places < fixed, places, passed)]].set(jnp.asarray(sizes, jnp.int32))

    sizes = jnp.where(number % 4 == 0, named(heavy_load, number // 4), named(usual, number - number // 4 - 1))
    mixed = jax.random.permutation(jax.random.fold_in(own, 3), number_of)
    donor, taker = mixed[0:number_of // 2 * 2:2], mixed[1:number_of // 2 * 2:2]
    room = jnp.minimum(sizes[donor] - 1, limit - sizes[taker]) // 2
    room = jnp.where((donor == ranking[0]) | (taker == ranking[0]) | (sizes[taker] == 0), 0, jnp.maximum(room, 0))
    passed = jax.random.randint(jax.random.fold_in(own, 4), (number_of // 2,), 0, 1 << 20) % (room + 1)
    sizes = sizes.at[donor].add(-passed).at[taker].add(passed)
    members = jnp.searchsorted(jnp.cumsum(sizes), jnp.arange(rows * top), side="right").astype(jnp.int32)
    grid = members.reshape(top, rows).T
    grid = grid[jax.random.permutation(jax.random.fold_in(own, 1), rows)]
    turn = jax.random.randint(jax.random.fold_in(own, 2), (rows, 1), 0, top)
    return jnp.take_along_axis(grid, (jnp.arange(top)[None, :] + turn) % top, axis=1)


def portions_of(amount, total, most, skew, full):
    loads = [(1 << 20) // math.isqrt(grade ** skew) + 1 for grade in range(1, amount + 1)]
    largest = most if full else min(most, max(-(-total // amount), total * loads[0] // sum(loads)))
    least = 1 if total - largest >= amount - 1 else 0
    holding, spare = [largest] + [least] * (amount - 1), total - largest - least * (amount - 1)
    while spare > 0:
        movable = [i for i in range(1, amount) if holding[i] < largest] or [i for i in range(1, amount) if holding[i] < most]
        mass, budget = sum([loads[i] for i in movable]), spare
        for i in movable:
            more = min(most - holding[i], max(1, budget * loads[i] // mass), spare)
            holding[i] = holding[i] + more
            spare = spare - more
    return np.array(holding)


def centred(stream_key, extent, scale, most, shards=(), kind=jnp.bfloat16):
    values = jax.random.normal(stream_key, extent, jnp.float32) * scale
    if len(shards) > 0:
        values = block_scale(stream_key, extent, shards, -0.22, 0.18) * values
    return jnp.clip(values, min=-most, max=most).astype(kind)


def setup_inputs(seed: int = 0, part: int = 0) -> dict:
    arg_keys = jax.random.split(jax.random.key(seed), 12)
    part_splits = jax.random.split(jax.random.fold_in(arg_keys[11], part), 12)
    acts = centred(part_splits[0], (TOKENS, D), 1.0, 6.0, ((0, 16),))
    grad_out = centred(part_splits[1], (TOKENS, KV), 1.0, 6.0, ((0, 16),))
    row_adapter_keys = jax.random.split(jax.random.fold_in(part_splits[2], 1), TOKENS // TOK_DEV)
    row_adapter_turns = jax.random.permutation(jax.random.fold_in(part_splits[2], 3), TOKENS // TOK_DEV)
    row_adapter = jax.vmap(lambda own, number: shared_out(jax.random.fold_in(part_splits[2], 2), own, number, TOK_DEV, ADAPTERS, 1, CAP, 2))(row_adapter_keys, row_adapter_turns).reshape((TOKENS, 1))
    ranks = plant(jax.random.randint(arg_keys[3], (ADAPTERS,), 8, R + 1), jax.random.fold_in(arg_keys[3], 1), 8, R).astype(jnp.int32)
    owner_map = jax.random.permutation(arg_keys[4], UNITS).astype(jnp.int32)
    down_slots = centred(part_splits[5], (UNITS, HALF, D), D ** -0.5, 0.0625, ((0, 16),), jnp.float32)
    up_slots = centred(part_splits[6], (UNITS, HALF, KV), KV ** -0.5, 0.1875, ((0, 16),), jnp.float32)
    down_first = centred(part_splits[7], (UNITS, HALF, D), 0.0002, 0.0029296875, ((0, 16),), jnp.float32)
    down_second = jnp.clip(jnp.exp(math.log(1.0000000116860974e-07) - 4.6051702 * jax.random.uniform(part_splits[8], (UNITS, HALF, D), jnp.float32) ** block_scale(part_splits[8], (UNITS, HALF, D), ((0, 16),), -0.2, 0.2)), 9.999999717180685e-10, 1.0000000116860974e-07)
    up_first = centred(part_splits[9], (UNITS, HALF, KV), 0.0002, 0.0029296875, ((0, 16),), jnp.float32)
    up_second = jnp.clip(jnp.exp(math.log(1.0000000116860974e-07) - 4.6051702 * jax.random.uniform(part_splits[10], (UNITS, HALF, KV), jnp.float32) ** block_scale(part_splits[10], (UNITS, HALF, KV), ((0, 16),), -0.2, 0.2)), 9.999999717180685e-10, 1.0000000116860974e-07)
    return {"acts": acts, "grad_out": grad_out, "row_adapter": row_adapter, "ranks": ranks, "owner_map": owner_map, "down_slots": down_slots, "up_slots": up_slots, "down_first": down_first, "down_second": down_second, "up_first": up_first, "up_second": up_second}


adapter_alpha_value = 16.0
clip_limit = 1.0
norm_eps = 1e-06
beta_one = 0.9
beta_two = 0.999
bias_one = 0.9999734386011124
bias_two = 0.0952078528862904
learn_rate = 0.0002
decay_rate = 0.01
adam_eps = 1e-08

def adamw_update(params, moment, second, gradient, clip_factor):
    clipped = clip_factor * gradient
    moment = beta_one * moment + (1.0 - beta_one) * clipped
    second = beta_two * second + (1.0 - beta_two) * clipped * clipped
    params = params - learn_rate * (moment / bias_one / (jnp.sqrt(second / bias_two) + adam_eps) + decay_rate * params)
    return (params, moment, second)

def reference(acts, grad_out, row_adapter, ranks, owner_map, down_slots, up_slots, down_first, down_second, up_first, up_second):
    row_ids = row_adapter[:, 0].astype(jnp.int32)
    sort_order = jnp.argsort(row_ids, stable=True).astype(jnp.int32)
    sorted_ids = row_ids[sort_order]
    adapter_labels = jnp.arange(ADAPTERS, dtype=jnp.int32)
    row_counts = lax.optimization_barrier(jnp.sum((row_ids[:, None] == adapter_labels[None, :]).astype(jnp.int32), axis=0))
    row_starts = (jnp.cumsum(row_counts) - row_counts).astype(jnp.int32)
    most_rows = N_DP * CAP
    pad_acts = jnp.concatenate([acts[sort_order], jnp.zeros((most_rows, D), acts.dtype)], 0)
    pad_grads = jnp.concatenate([grad_out[sort_order], jnp.zeros((most_rows, KV), grad_out.dtype)], 0)
    columns = jnp.arange(HALF, dtype=jnp.int32)
    inner_rows = jnp.arange(most_rows, dtype=jnp.int32)

    def per_adapter(adapter):
        first_row = row_starts[adapter]
        live_rows = inner_rows < row_counts[adapter]
        row_block_list = lax.dynamic_slice(pad_acts, (first_row, jnp.int32(0)), (most_rows, D))
        row_block_list = jnp.where(live_rows[:, None], row_block_list, jnp.zeros_like(row_block_list))
        gradient_block_list = lax.dynamic_slice(pad_grads, (first_row, jnp.int32(0)), (most_rows, KV))
        gradient_block_list = jnp.where(live_rows[:, None], gradient_block_list, jnp.zeros_like(gradient_block_list))
        local_rank_value = ranks[adapter]
        adapter_scale_factor = adapter_alpha_value / local_rank_value.astype(jnp.float32)
        down_gradient_list = []
        up_gradient_list = []
        piece_list = []
        for half_idx in range(2):
            slot_id = owner_map[2 * adapter + half_idx]
            rank_keep = half_idx * HALF + columns < local_rank_value
            down_weight_bf16 = jnp.where(rank_keep[:, None], down_slots[slot_id], 0.0).astype(jnp.bfloat16)
            up_weight_bf16 = jnp.where(rank_keep[:, None], up_slots[slot_id], 0.0).astype(jnp.bfloat16)
            hidden_state = jnp.dot(row_block_list, down_weight_bf16.T, preferred_element_type=jnp.float32).astype(jnp.bfloat16)
            lowrank_gradient = jnp.dot(gradient_block_list, up_weight_bf16.T, preferred_element_type=jnp.float32).astype(jnp.bfloat16)
            up_gradient_list.append(adapter_scale_factor * jnp.dot(hidden_state.T, gradient_block_list, preferred_element_type=jnp.float32))
            down_gradient_list.append(adapter_scale_factor * jnp.dot(lowrank_gradient.T, row_block_list, preferred_element_type=jnp.float32))
            piece_list.append((adapter_scale_factor * jnp.dot(lowrank_gradient, down_weight_bf16, preferred_element_type=jnp.float32)).astype(jnp.bfloat16))
        joined = (piece_list[0].astype(jnp.float32) + piece_list[1].astype(jnp.float32)).astype(jnp.bfloat16)
        return (jnp.stack(down_gradient_list), jnp.stack(up_gradient_list), joined)
    down_gradient, up_gradient, joined = lax.map(per_adapter, adapter_labels)
    position = jnp.arange(TOKENS, dtype=jnp.int32) - row_starts[sorted_ids]
    sorted_grad = joined[sorted_ids, position]
    inverse = jnp.argsort(sort_order).astype(jnp.int32)
    input_grad = sorted_grad[inverse]
    unit_of_slot = jnp.argsort(owner_map).astype(jnp.int32)
    down_gradient = down_gradient.reshape(UNITS, HALF, D)[unit_of_slot]
    up_gradient = up_gradient.reshape(UNITS, HALF, KV)[unit_of_slot]
    squares_sum = jnp.sum(down_gradient * down_gradient) + jnp.sum(up_gradient * up_gradient)
    clip_factor = jnp.minimum(1.0, clip_limit / (jnp.sqrt(squares_sum) + norm_eps))
    new_down, new_down_first, new_down_second = adamw_update(down_slots, down_first, down_second, down_gradient, clip_factor)
    new_up, new_up_first, new_up_second = adamw_update(up_slots, up_first, up_second, up_gradient, clip_factor)
    return (input_grad, new_down, new_up, new_down_first, new_down_second, new_up_first, new_up_second)
```

```python
import jax
import jax.numpy as jnp
from jax import lax
from jax.sharding import PartitionSpec as P

adapter_alpha_value = 16.0
clip_limit = 1.0
norm_eps = 1e-06
beta_one = 0.9
beta_two = 0.999
bias_one = 0.9999734386011124
bias_two = 0.0952078528862904
learn_rate = 0.0002
decay_rate = 0.01
adam_eps = 1e-08


def adamw_update(params, moment, second, gradient, clip_factor):
    clipped = clip_factor * gradient
    moment = beta_one * moment + (1.0 - beta_one) * clipped
    second = beta_two * second + (1.0 - beta_two) * clipped * clipped
    params = params - learn_rate * (
        moment / bias_one / (jnp.sqrt(second / bias_two) + adam_eps) + decay_rate * params
    )
    return (params, moment, second)


def on_device(
    acts,
    grad_out,
    row_adapter,
    ranks,
    owner_map,
    down_slots,
    up_slots,
    down_first,
    down_second,
    up_first,
    up_second,
):
    rows, width = acts.shape
    out_width = grad_out.shape[1]
    devices = lax.axis_size("dp")
    own, depth = down_slots.shape[0], down_slots.shape[1]
    slots = owner_map.shape[0]
    halves = 2
    team = devices // halves
    cut = width // team
    out_cut = out_width // team
    half_slots = own * team
    cols = half_slots * depth
    all_rows = devices * rows
    groups = [[h * team + j for j in range(team)] for h in range(halves)]
    me = lax.axis_index("dp")
    f32, bf16 = jnp.float32, jnp.bfloat16

    unit_labels = jnp.arange(slots, dtype=jnp.int32)
    adapter_labels = jnp.arange(ranks.shape[0], dtype=jnp.int32)

    def describe(first_slot, count):
        here = first_slot + jnp.arange(count, dtype=jnp.int32)
        unit = jnp.sum(jnp.where(owner_map[None, :] == here[:, None], unit_labels[None, :], 0), axis=1)
        rank = jnp.sum(
            jnp.where(adapter_labels[None, :] == (unit // 2)[:, None], ranks[None, :], 0), axis=1
        )
        return unit, rank

    own_unit, own_rank = describe(me * own, own)
    keep = (own_unit % 2)[:, None] * depth + jnp.arange(depth, dtype=jnp.int32)[None, :] < own_rank[:, None]
    keep = keep.reshape(own * depth, 1)
    down_flat = down_slots.reshape(own * depth, width)
    up16 = jnp.where(keep, up_slots.reshape(own * depth, out_width), 0.0).astype(bf16)
    seat = me % team
    team_perms = [[(i, i ^ b) for i in range(devices)] for b in range(team)]

    def sliced(array, pieces):
        return array.reshape(array.shape[0], pieces, -1).transpose(1, 0, 2)

    def to_team(array):
        return lax.all_to_all(array, "dp", split_axis=0, concat_axis=0, axis_index_groups=groups, tiled=True)

    def to_all(array):
        return lax.all_to_all(array, "dp", split_axis=0, concat_axis=0, tiled=True)

    def swap(blocks):
        return [blocks[0]] + [lax.ppermute(blocks[b], "dp", team_perms[b]) for b in range(1, team)]

    def double(array, span, wide):
        step = 1
        while step < span:
            sent = array if wide or step == 1 else array.astype(bf16)
            got = lax.ppermute(sent, "dp", [(i, i ^ step) for i in range(devices)])
            array = sent.astype(f32) + got.astype(f32)
            step *= 2
        return array

    id_rows = -(-rows // out_cut)
    id_block = jnp.pad(row_adapter[:, 0], (0, id_rows * out_cut - rows)).astype(bf16)
    id_block = jnp.pad(id_block.reshape(id_rows, out_cut), ((0, -id_rows % 16), (0, 0)))
    g_send = jnp.concatenate(
        [sliced(grad_out, team), jnp.broadcast_to(id_block, (team,) + id_block.shape)], axis=1
    )
    g_got = to_all(jnp.tile(g_send, (halves, 1, 1)))
    g_cut = g_got[:, :rows].reshape(all_rows, out_cut)
    ids = g_got[:, rows : rows + id_rows].reshape(devices, -1)[:, :rows].reshape(all_rows)
    ids = ids.astype(f32).astype(jnp.int32)
    b_cut = to_team(sliced(up16, team)).reshape(cols, out_cut)
    acts_now, _, _ = lax.optimization_barrier((acts, g_got, b_cut))
    x_cut = to_all(jnp.tile(sliced(acts_now, team), (halves, 1, 1))).reshape(all_rows, cut)
    a_blocks = []
    for b in range(team):
        part = lax.dynamic_slice_in_dim(down_flat, (seat ^ b) * cut, cut, axis=1)
        a_blocks.append(jnp.where(keep, part, 0.0).astype(bf16))
    a_cut = jnp.concatenate(swap(a_blocks), axis=0)

    half_unit, half_rank = describe(me // team * half_slots, half_slots)
    seats = jnp.arange(team, dtype=jnp.int32) ^ seat

    def columns(reorder):
        unit, rank = half_unit, half_rank
        if reorder:
            unit = jnp.take(unit.reshape(team, own), seats, axis=0).reshape(-1)
            rank = jnp.take(rank.reshape(team, own), seats, axis=0).reshape(-1)
        unit = jnp.repeat(unit, depth)
        scale = adapter_alpha_value / jnp.repeat(rank, depth).astype(f32)
        lane = unit % 2 * depth + jnp.arange(cols, dtype=jnp.int32) % depth
        fold = (lane[None, :] == jnp.arange(2 * depth, dtype=jnp.int32)[:, None]).astype(bf16)
        match = ids[:, None] == (unit // 2)[None, :]
        return scale, fold, match

    b_side, a_side = columns(False), columns(True)

    def narrow(left, right, side):
        _, fold, match = side
        product = lax.dot_general(left, right, (((1,), (1,)), ((), ())), preferred_element_type=f32)
        masked = jnp.where(match, product, 0.0).astype(bf16)
        part = lax.dot_general(fold, masked, (((1,), (1,)), ((), ())), preferred_element_type=f32)
        return double(part, team, False).astype(bf16)

    def widen(lanes, side):
        _, fold, match = side
        spread = lax.dot_general(lanes, fold, (((0,), (0,)), ((), ())), preferred_element_type=f32)
        return jnp.where(match, spread, 0.0).astype(bf16)

    low = widen(narrow(g_cut, b_cut, b_side), a_side)
    piece = jnp.dot(low, a_cut, preferred_element_type=f32).astype(bf16)
    back = to_all(piece.reshape(devices, rows, cut)).astype(f32)

    x_late, _ = lax.optimization_barrier((x_cut, piece))
    hidden = widen(narrow(x_late, a_cut, a_side), b_side)
    down_parts, squares = [], jnp.zeros((), f32)
    for b in range(team):
        span = slice(b * own * depth, (b + 1) * own * depth)
        part = a_side[0][span, None] * lax.dot_general(
            low[:, span], x_late, (((0,), (0,)), ((), ())), preferred_element_type=f32
        )
        squares = squares + jnp.sum(part * part)
        down_parts.append(part.astype(bf16))
    down_parts = swap(down_parts)
    up_grad = b_side[0][:, None] * lax.dot_general(
        hidden, g_cut, (((0,), (0,)), ((), ())), preferred_element_type=f32
    )
    squares = double(squares + jnp.sum(up_grad * up_grad), devices, True)
    clip_factor = jnp.minimum(1.0, clip_limit / (jnp.sqrt(squares) + norm_eps))
    up_parts = swap(
        [
            lax.dynamic_slice_in_dim(up_grad.astype(bf16), (seat ^ b) * own * depth, own * depth, axis=0)
            for b in range(team)
        ]
    )

    def home(parts, part_width, whole_width):
        grad = jnp.zeros((own * depth, whole_width), bf16)
        for b in range(team):
            grad = lax.dynamic_update_slice_in_dim(grad, parts[b], (seat ^ b) * part_width, axis=1)
        return grad.reshape(own, depth, whole_width).astype(f32)

    down_new = adamw_update(down_slots, down_first, down_second, home(down_parts, cut, width), clip_factor)
    up_new = adamw_update(up_slots, up_first, up_second, home(up_parts, out_cut, out_width), clip_factor)

    row_rank = jnp.sum(jnp.where(row_adapter == adapter_labels[None, :], ranks[None, :], 0), axis=1)
    row_scale = adapter_alpha_value / row_rank.astype(f32)
    joined = (back[:team] + back[team:]).transpose(1, 0, 2).reshape(rows, width)
    input_grad = (row_scale[:, None] * joined).astype(bf16)
    return (input_grad, down_new[0], up_new[0], down_new[1], down_new[2], up_new[1], up_new[2])


def solution(mesh):
    two = P(("groups", "dp"), None)
    three = P(("groups", "dp"), None, None)
    return jax.shard_map(
        on_device,
        mesh=mesh,
        in_specs=(two, two, two, P(), P(), three, three, three, three, three, three),
        out_specs=(two, three, three, three, three, three, three),
        check_vma=False,
    )
```

```python
import jax
import jax.numpy as jnp
from jax import lax
from jax.experimental import pallas as pl
from jax.experimental.pallas import tpu as pltpu
from jax.sharding import PartitionSpec as P

adapter_alpha_value = 16.0
clip_limit = 1.0
norm_eps = 1e-06
beta_one = 0.9
beta_two = 0.999
bias_one = 0.9999734386011124
bias_two = 0.0952078528862904
learn_rate = 0.0002
decay_rate = 0.01
adam_eps = 1e-08


def adamw_update(params, moment, second, gradient, clip_factor):
    clipped = clip_factor * gradient
    moment = beta_one * moment + (1.0 - beta_one) * clipped
    second = beta_two * second + (1.0 - beta_two) * clipped * clipped
    params = params - learn_rate * (
        moment / bias_one / (jnp.sqrt(second / bias_two) + adam_eps) + decay_rate * params
    )
    return (params, moment, second)


ROOM = pltpu.CompilerParams(vmem_limit_bytes=28 * 1024 * 1024)
NT = (((1,), (1,)), ((), ()))
TN = (((0,), (0,)), ((), ()))


def whole(array):
    return pl.BlockSpec(array.shape, lambda *_: (0,) * array.ndim)


def cost(flops, size):
    return pl.CostEstimate(flops=flops // 4096, bytes_accessed=size // 4096, transcendentals=0)


def narrow(units, ids, left, stacks, places, depth):
    rows, span = left.shape
    size = stacks[0].shape[1]
    tile = min(rows, 256)

    def kernel(units_ref, ids_ref, left_ref, *refs):
        out_ref = refs[-1]
        twice = 2 * ids_ref[...]
        first = jnp.zeros((depth, tile), jnp.float32)
        second = first
        for c, (stack, place) in enumerate(places):
            product = lax.dot_general(refs[stack][place], left_ref[...], NT, preferred_element_type=jnp.float32)
            for k in range(size // depth):
                unit = units_ref[c * (size // depth) + k]
                lanes = product[k * depth : (k + 1) * depth]
                first = first + jnp.where(twice == unit, lanes, 0.0)
                second = second + jnp.where(twice + 1 == unit, lanes, 0.0)
        out_ref[:depth, :] = first
        out_ref[depth:, :] = second

    return pl.pallas_call(
        kernel,
        grid_spec=pltpu.PrefetchScalarGridSpec(
            num_scalar_prefetch=1,
            grid=(rows // tile,),
            in_specs=[
                pl.BlockSpec((1, tile), lambda i, _: (0, i)),
                pl.BlockSpec((tile, span), lambda i, _: (i, 0)),
            ]
            + [whole(stack) for stack in stacks],
            out_specs=pl.BlockSpec((2 * depth, tile), lambda i, _: (0, i)),
        ),
        out_shape=jax.ShapeDtypeStruct((2 * depth, rows), jnp.float32),
        compiler_params=ROOM,
        cost_estimate=cost(2 * rows * size * len(places) * span, 2 * rows * span),
        name="narrow",
    )(units, ids, left, *stacks)


def spread(unit, twice, lanes, depth):
    second = jnp.where(twice + 1 == unit, lanes[depth:], 0.0)
    return jnp.where(twice == unit, lanes[:depth], second).astype(jnp.bfloat16)


def pieces_of(units, ids, lanes, stacks, places, depth):
    rows = lanes.shape[1]
    _, size, span = stacks[0].shape
    tile = min(rows, 256)

    def kernel(units_ref, ids_ref, lanes_ref, *refs):
        out_ref, wide = refs[-2:]
        twice = 2 * ids_ref[...]
        total = jnp.zeros((tile, span), jnp.float32)
        for c, (stack, place) in enumerate(places):
            for k in range(size // depth):
                unit = units_ref[c * (size // depth) + k]
                wide[c, k * depth : (k + 1) * depth, :] = spread(unit, twice, lanes_ref[...], depth)
            total = total + lax.dot_general(
                wide[c], refs[stack][place], TN, preferred_element_type=jnp.float32
            )
        out_ref[...] = total.astype(out_ref.dtype)

    return pl.pallas_call(
        kernel,
        grid_spec=pltpu.PrefetchScalarGridSpec(
            num_scalar_prefetch=1,
            grid=(rows // tile,),
            in_specs=[
                pl.BlockSpec((1, tile), lambda i, _: (0, i)),
                pl.BlockSpec((2 * depth, tile), lambda i, _: (0, i)),
            ]
            + [whole(stack) for stack in stacks],
            out_specs=pl.BlockSpec((tile, span), lambda i, _: (i, 0)),
            scratch_shapes=[pltpu.VMEM((len(places), size, tile), jnp.bfloat16)],
        ),
        out_shape=jax.ShapeDtypeStruct((rows, span), jnp.bfloat16),
        compiler_params=ROOM,
        cost_estimate=cost(2 * rows * size * len(places) * span, 2 * rows * span),
        name="pieces",
    )(units, ids, lanes, *stacks)


def gradient(units, ids, lanes, right, scale, parts, depth):
    rows, span = right.shape
    cols = scale.shape[0]
    size = cols // parts

    def kernel(units_ref, ids_ref, lanes_ref, right_ref, scale_ref, out_ref, square_ref, wide):
        b = pl.program_id(0)
        twice = 2 * ids_ref[...]
        for u in range(size // depth):
            wide[u * depth : (u + 1) * depth, :] = spread(
                units_ref[b * (size // depth) + u], twice, lanes_ref[...], depth
            )
        grad = scale_ref[...] * jnp.dot(wide[...], right_ref[...], preferred_element_type=jnp.float32)
        out_ref[0] = grad.astype(out_ref.dtype)

        @pl.when(b == 0)
        def _():
            square_ref[...] = jnp.zeros_like(square_ref)

        square_ref[...] += jnp.sum(grad * grad, axis=0, keepdims=True)

    return pl.pallas_call(
        kernel,
        grid_spec=pltpu.PrefetchScalarGridSpec(
            num_scalar_prefetch=1,
            grid=(parts,),
            in_specs=[
                whole(ids),
                whole(lanes),
                whole(right),
                pl.BlockSpec((size, 1), lambda i, _: (i, 0)),
            ],
            out_specs=[
                pl.BlockSpec((1, size, span), lambda i, _: (i, 0, 0)),
                pl.BlockSpec((1, span), lambda i, _: (0, 0)),
            ],
            scratch_shapes=[pltpu.VMEM((size, rows), jnp.bfloat16)],
        ),
        out_shape=[
            jax.ShapeDtypeStruct((parts, size, span), jnp.bfloat16),
            jax.ShapeDtypeStruct((1, span), jnp.float32),
        ],
        compiler_params=ROOM,
        cost_estimate=cost(2 * rows * cols * span, 2 * (rows + cols) * span),
        name="gradient",
    )(units, ids, lanes, right, scale.reshape(cols, 1))


def update_slots(params, moment, second, stacks, places, columns, clip_factor):
    count = len(places)
    _, rows, cut = stacks[0].shape
    width = count * cut
    tile = min(rows, max(16, 131072 // cut))

    def kernel(columns_ref, clip_ref, p_ref, m_ref, v_ref, *refs):
        new_p_ref, new_m_ref, new_v_ref, grad = refs[-4:]
        c, i = pl.program_id(0), pl.program_id(1)
        start = pl.multiple_of(i * tile, tile)
        for k, (stack, place) in enumerate(places):

            @pl.when(c == k)
            def _():
                grad[...] = refs[stack][place, pl.ds(start, tile), :].astype(jnp.float32)

        new = adamw_update(p_ref[...], m_ref[...], v_ref[...], grad[...], clip_ref[0, 0])
        new_p_ref[...], new_m_ref[...], new_v_ref[...] = new

    block = pl.BlockSpec((tile, cut), lambda c, i, columns_ref: (i, columns_ref[c]))
    shape = jax.ShapeDtypeStruct((rows, width), jnp.float32)
    new = pl.pallas_call(
        kernel,
        grid_spec=pltpu.PrefetchScalarGridSpec(
            num_scalar_prefetch=1,
            grid=(count, rows // tile),
            in_specs=[pl.BlockSpec(memory_space=pltpu.SMEM)] + [block] * 3 + [whole(stack) for stack in stacks],
            out_specs=[block] * 3,
            scratch_shapes=[pltpu.VMEM((tile, cut), jnp.float32)],
        ),
        out_shape=[shape] * 3,
        compiler_params=ROOM,
        cost_estimate=cost(20 * rows * width, 26 * rows * width),
        name="update",
    )(columns, clip_factor.reshape(1, 1), *[a.reshape(rows, width) for a in (params, moment, second)], *stacks)
    return [a.reshape(params.shape) for a in new]


def join(back, scale, team):
    _, rows, cut = back.shape

    def kernel(one_ref, two_ref, scale_ref, out_ref):
        total = one_ref[0].astype(jnp.float32) + two_ref[0].astype(jnp.float32)
        out_ref[...] = (scale_ref[...] * total).astype(out_ref.dtype)

    return pl.pallas_call(
        kernel,
        grid=(team,),
        in_specs=[
            pl.BlockSpec((1, rows, cut), lambda j: (j, 0, 0)),
            pl.BlockSpec((1, rows, cut), lambda j: (team + j, 0, 0)),
            pl.BlockSpec((rows, 1), lambda j: (0, 0)),
        ],
        out_specs=pl.BlockSpec((rows, cut), lambda j: (0, j)),
        out_shape=jax.ShapeDtypeStruct((rows, team * cut), back.dtype),
        compiler_params=ROOM,
        cost_estimate=cost(3 * rows * team * cut, 6 * rows * team * cut),
        name="join",
    )(back, back, scale)


def on_device(
    acts,
    grad_out,
    row_adapter,
    ranks,
    owner_map,
    down_slots,
    up_slots,
    down_first,
    down_second,
    up_first,
    up_second,
):
    rows, width = acts.shape
    out_width = grad_out.shape[1]
    devices = lax.axis_size("dp")
    own, depth = down_slots.shape[0], down_slots.shape[1]
    slots = owner_map.shape[0]
    halves = 2
    team = devices // halves
    cut = width // team
    out_cut = out_width // team
    half_slots = own * team
    all_rows = devices * rows
    span = own * depth
    me = lax.axis_index("dp")
    seat = me % team
    f32, bf16 = jnp.float32, jnp.bfloat16

    unit_labels = jnp.arange(slots, dtype=jnp.int32)
    adapter_labels = jnp.arange(ranks.shape[0], dtype=jnp.int32)

    def describe(first_slot, count):
        here = first_slot + jnp.arange(count, dtype=jnp.int32)
        unit = jnp.sum(jnp.where(owner_map[None, :] == here[:, None], unit_labels[None, :], 0), axis=1)
        rank = jnp.sum(
            jnp.where(adapter_labels[None, :] == (unit // 2)[:, None], ranks[None, :], 0), axis=1
        )
        return unit, rank

    own_unit, own_rank = describe(me * own, own)
    keep = (own_unit % 2)[:, None] * depth + jnp.arange(depth, dtype=jnp.int32)[None, :] < own_rank[:, None]
    keep = keep.reshape(span, 1)
    down_flat = down_slots.reshape(span, width)
    up16 = jnp.where(keep, up_slots.reshape(span, out_width), 0.0).astype(bf16)

    def sliced(array, pieces):
        return array.reshape(array.shape[0], pieces, -1).transpose(1, 0, 2)

    def to_all(array):
        return lax.all_to_all(array, "dp", split_axis=0, concat_axis=0, tiled=True)

    core = seat % 2
    order = list(range(0, team, 2)) + list(range(1, team, 2))
    peers = [seat ^ b for b in order]

    def to_team(array):
        groups = [[h * team + j for j in range(team)] for h in range(halves)]
        return lax.all_to_all(array, "dp", split_axis=0, concat_axis=0, axis_index_groups=groups, tiled=True)

    def send(array, apart):
        return lax.ppermute(array, "dp", [(i, i ^ apart) for i in range(devices)])

    def swap(blocks, beside, packed=False):
        count = team // 2
        got, beside = lax.optimization_barrier((send(jnp.stack(blocks[count:]), 1), beside))
        pairs = [jnp.stack([blocks[k], got[k]]) for k in range(1, count)]
        if packed:
            pairs, beside = lax.optimization_barrier((pairs, beside))
        return beside, [blocks[0][None], got] + [send(pair, b) for pair, b in zip(pairs, order[1:])]

    def swap_back(parts):
        count = team // 2
        pairs = [send(parts[2 * k : 2 * k + 2], 2 * k) for k in range(1, count)]
        got = send(jnp.stack([parts[1]] + [pair[1] for pair in pairs]), 1)
        return [parts[:1]] + pairs + [got]

    places = [(0, 0)] + [(k + 1, 0) for k in range(1, team // 2)]
    places = places + [(1, 0)] + [(k + 1, 1) for k in range(1, team // 2)]

    def chip_sum(part):
        return part + send(part, 1)

    def team_sum(chip, beside):
        half = chip.shape[1] // 2
        mine = lax.dynamic_slice_in_dim(chip, core * half, half, axis=1)
        step = 2
        while step < team:
            other, beside = lax.optimization_barrier((send(mine.astype(bf16), step), beside))
            mine = mine + other.astype(f32)
            step *= 2
        mine = mine.astype(bf16)
        other = send(mine, 1)
        even = core == 0
        both = [jnp.where(even, mine, other), jnp.where(even, other, mine)]
        return jnp.concatenate(both, axis=1).astype(f32), beside

    def double(array):
        step = 1
        while step < devices:
            array = array + send(array, step)
            step *= 2
        return array

    def columns_of(array, peer, size):
        return lax.dynamic_slice_in_dim(array, peer * size, size, axis=1)

    id_rows = -(-rows // out_cut)
    id_block = jnp.pad(row_adapter[:, 0], (0, id_rows * out_cut - rows)).astype(bf16)
    id_block = jnp.pad(id_block.reshape(id_rows, out_cut), ((0, -id_rows % 16), (0, 0)))
    tall = rows + id_block.shape[0]
    g_and_b = jnp.concatenate([grad_out, jnp.tile(id_block, (1, team)), up16], axis=0)
    _, stacks = swap([columns_of(g_and_b, peer, out_cut) for peer in peers], ())
    blocks = [stacks[stack][place] for stack, place in places]
    mine = jnp.zeros((team * tall, out_cut), bf16)
    for peer, block in zip(peers, blocks):
        mine = lax.dynamic_update_slice_in_dim(mine, block[:tall], peer * tall, axis=0)
    b_cut = jnp.stack([block[tall:] for block in blocks])
    theirs = lax.ppermute(mine, "dp", [(i, (i + team) % devices) for i in range(devices)])
    lower = me < team
    g_got = jnp.concatenate([jnp.where(lower, mine, theirs), jnp.where(lower, theirs, mine)], axis=0)
    g_got = g_got.reshape(devices, tall, out_cut)
    g_cut = g_got[:, :rows].reshape(all_rows, out_cut)
    ids = g_got[:, rows : rows + id_rows].reshape(devices, -1)[:, :rows].reshape(1, all_rows)
    ids = ids.astype(f32).astype(jnp.int32)

    half_unit, half_rank = describe(me // team * half_slots, half_slots)
    seats = jnp.stack(peers)
    units = jnp.take(half_unit.reshape(team, own), seats, axis=0).reshape(-1)
    unit_rank = jnp.take(half_rank.reshape(team, own), seats, axis=0).reshape(-1)
    col_scale = adapter_alpha_value / jnp.repeat(unit_rank, depth).astype(f32)
    pair_seats = jnp.arange(team, dtype=jnp.int32) ^ seat
    pair_units = jnp.take(half_unit.reshape(team, own), pair_seats, axis=0).reshape(-1)
    pair_rank = jnp.take(half_rank.reshape(team, own), pair_seats, axis=0).reshape(-1)
    pair_scale = adapter_alpha_value / jnp.repeat(pair_rank, depth).astype(f32)
    half_scale = adapter_alpha_value / jnp.repeat(half_rank, depth).astype(f32)

    acts_send = jnp.tile(sliced(acts, team), (halves, 1, 1))
    acts_send, g_cut = lax.optimization_barrier((acts_send, g_cut))
    x_cut = to_all(acts_send).reshape(all_rows, cut)
    alone = [(0, k) for k in range(team)]
    low_chip = chip_sum(narrow(units, ids, g_cut, [b_cut], alone, depth))
    low_chip, down_late = lax.optimization_barrier((low_chip, down_flat))
    a_blocks = [jnp.where(keep, columns_of(down_late, peer, cut), 0.0).astype(bf16) for peer in peers]
    low_chip, a_stacks = swap(a_blocks, low_chip)
    low, _ = team_sum(low_chip, ids)
    down_parts, down_squares = gradient(pair_units, ids, low, x_cut, pair_scale, team, depth)
    down_stacks = swap_back(down_parts)
    down_places = [(k, 0) for k in range(team // 2)] + [(team // 2, k) for k in range(team // 2)]
    x_late, a_stacks, _ = lax.optimization_barrier((x_cut, a_stacks, down_parts))
    hidden_part = narrow(units, ids, x_late, a_stacks, places, depth)
    hidden_chip, a_stacks = lax.optimization_barrier((chip_sum(hidden_part), a_stacks))
    piece = pieces_of(units, ids, low, a_stacks, places, depth)
    hidden, piece = team_sum(hidden_chip, piece)
    up_parts, up_squares = gradient(half_unit, ids, hidden, g_cut, half_scale, team, depth)
    up_home = to_team(up_parts)
    squares = double(jnp.sum(down_squares) + jnp.sum(up_squares))
    clip_factor = jnp.minimum(1.0, clip_limit / (jnp.sqrt(squares) + norm_eps))
    piece, _, down_stacks, up_home = lax.optimization_barrier((piece, squares, down_stacks, up_home))
    back = to_all(piece.reshape(devices, rows, cut))
    columns = jnp.stack(peers)
    down_new = update_slots(down_slots, down_first, down_second, down_stacks, down_places, columns, clip_factor)
    up_grad = up_home.transpose(1, 0, 2).reshape(own, depth, out_width).astype(f32)
    up_new = adamw_update(up_slots, up_first, up_second, up_grad, clip_factor)

    row_rank = jnp.sum(jnp.where(row_adapter == adapter_labels[None, :], ranks[None, :], 0), axis=1)
    input_grad = join(back, (adapter_alpha_value / row_rank.astype(f32))[:, None], team)
    return (input_grad, down_new[0], up_new[0], down_new[1], down_new[2], up_new[1], up_new[2])


def solution(mesh):
    two = P(("groups", "dp"), None)
    three = P(("groups", "dp"), None, None)
    return jax.shard_map(
        on_device,
        mesh=mesh,
        in_specs=(two, two, two, P(), P(), three, three, three, three, three, three),
        out_specs=(two, three, three, three, three, three, three),
        check_vma=False,
    )
```

```python
import jax
import jax.numpy as jnp
from jax import lax
from jax.experimental import pallas as pl
from jax.experimental.pallas import tpu as pltpu
from jax.sharding import PartitionSpec as P

adapter_alpha_value = 16.0
clip_limit = 1.0
norm_eps = 1e-06
beta_one = 0.9
beta_two = 0.999
bias_one = 0.9999734386011124
bias_two = 0.0952078528862904
learn_rate = 0.0002
decay_rate = 0.01
adam_eps = 1e-08


def adamw_update(params, moment, second, gradient, clip_factor):
    clipped = clip_factor * gradient
    moment = beta_one * moment + (1.0 - beta_one) * clipped
    second = beta_two * second + (1.0 - beta_two) * clipped * clipped
    params = params - learn_rate * (
        moment / bias_one / (jnp.sqrt(second / bias_two) + adam_eps) + decay_rate * params
    )
    return (params, moment, second)


ROOM = pltpu.CompilerParams(vmem_limit_bytes=28 * 1024 * 1024)
NT = (((1,), (1,)), ((), ()))
TN = (((0,), (0,)), ((), ()))


def whole(array):
    return pl.BlockSpec(array.shape, lambda *_: (0,) * array.ndim)


def cost(flops, size):
    return pl.CostEstimate(flops=flops // 4096, bytes_accessed=size // 4096, transcendentals=0)


def narrow(units, ids, left, stacks, places, depth):
    rows, span = left.shape
    size = stacks[0].shape[1]
    tile = min(rows, 512)

    def kernel(units_ref, ids_ref, left_ref, *refs):
        out_ref = refs[-1]
        twice = 2 * ids_ref[...]
        first = jnp.zeros((depth, tile), jnp.float32)
        second = first
        for c, (stack, place) in enumerate(places):
            product = lax.dot_general(refs[stack][place], left_ref[...], NT, preferred_element_type=jnp.float32)
            for k in range(size // depth):
                unit = units_ref[c * (size // depth) + k]
                lanes = product[k * depth : (k + 1) * depth]
                first = first + jnp.where(twice == unit, lanes, 0.0)
                second = second + jnp.where(twice + 1 == unit, lanes, 0.0)
        out_ref[:depth, :] = first
        out_ref[depth:, :] = second

    return pl.pallas_call(
        kernel,
        grid_spec=pltpu.PrefetchScalarGridSpec(
            num_scalar_prefetch=1,
            grid=(rows // tile,),
            in_specs=[
                pl.BlockSpec((1, tile), lambda i, _: (0, i)),
                pl.BlockSpec((tile, span), lambda i, _: (i, 0)),
            ]
            + [whole(stack) for stack in stacks],
            out_specs=pl.BlockSpec((2 * depth, tile), lambda i, _: (0, i)),
        ),
        out_shape=jax.ShapeDtypeStruct((2 * depth, rows), jnp.float32),
        compiler_params=ROOM,
        cost_estimate=cost(2 * rows * size * len(places) * span, 2 * rows * span),
        name="narrow",
    )(units, ids, left, *stacks)


def spread(unit, twice, lanes, depth):
    second = jnp.where(twice + 1 == unit, lanes[depth:], 0.0)
    return jnp.where(twice == unit, lanes[:depth], second).astype(jnp.bfloat16)


def pieces_of(units, ids, lanes, stacks, places, depth):
    rows = lanes.shape[1]
    _, size, span = stacks[0].shape
    tile = min(rows, 512)

    def kernel(units_ref, ids_ref, lanes_ref, *refs):
        out_ref, wide = refs[-2:]
        twice = 2 * ids_ref[...]
        total = jnp.zeros((tile, span), jnp.float32)
        for c, (stack, place) in enumerate(places):
            for k in range(size // depth):
                unit = units_ref[c * (size // depth) + k]
                wide[c, k * depth : (k + 1) * depth, :] = spread(unit, twice, lanes_ref[...], depth)
            total = total + lax.dot_general(
                wide[c], refs[stack][place], TN, preferred_element_type=jnp.float32
            )
        out_ref[...] = total.astype(out_ref.dtype)

    return pl.pallas_call(
        kernel,
        grid_spec=pltpu.PrefetchScalarGridSpec(
            num_scalar_prefetch=1,
            grid=(rows // tile,),
            in_specs=[
                pl.BlockSpec((1, tile), lambda i, _: (0, i)),
                pl.BlockSpec((2 * depth, tile), lambda i, _: (0, i)),
            ]
            + [whole(stack) for stack in stacks],
            out_specs=pl.BlockSpec((tile, span), lambda i, _: (i, 0)),
            scratch_shapes=[pltpu.VMEM((len(places), size, tile), jnp.bfloat16)],
        ),
        out_shape=jax.ShapeDtypeStruct((rows, span), jnp.bfloat16),
        compiler_params=ROOM,
        cost_estimate=cost(2 * rows * size * len(places) * span, 2 * rows * span),
        name="pieces",
    )(units, ids, lanes, *stacks)


def gradient(units, ids, lanes, right, scale, parts, depth):
    rows, span = right.shape
    cols = scale.shape[0]
    size = cols // parts

    def kernel(units_ref, ids_ref, lanes_ref, right_ref, scale_ref, out_ref, square_ref, wide):
        b = pl.program_id(0)
        twice = 2 * ids_ref[...]
        for u in range(size // depth):
            wide[u * depth : (u + 1) * depth, :] = spread(
                units_ref[b * (size // depth) + u], twice, lanes_ref[...], depth
            )
        grad = scale_ref[...] * jnp.dot(wide[...], right_ref[...], preferred_element_type=jnp.float32)
        out_ref[0] = grad.astype(out_ref.dtype)

        @pl.when(b == 0)
        def _():
            square_ref[...] = jnp.zeros_like(square_ref)

        square_ref[...] += jnp.sum(grad * grad, axis=0, keepdims=True)

    return pl.pallas_call(
        kernel,
        grid_spec=pltpu.PrefetchScalarGridSpec(
            num_scalar_prefetch=1,
            grid=(parts,),
            in_specs=[
                whole(ids),
                whole(lanes),
                whole(right),
                pl.BlockSpec((size, 1), lambda i, _: (i, 0)),
            ],
            out_specs=[
                pl.BlockSpec((1, size, span), lambda i, _: (i, 0, 0)),
                pl.BlockSpec((1, span), lambda i, _: (0, 0)),
            ],
            scratch_shapes=[pltpu.VMEM((size, rows), jnp.bfloat16)],
        ),
        out_shape=[
            jax.ShapeDtypeStruct((parts, size, span), jnp.bfloat16),
            jax.ShapeDtypeStruct((1, span), jnp.float32),
        ],
        compiler_params=ROOM,
        cost_estimate=cost(2 * rows * cols * span, 2 * (rows + cols) * span),
        name="gradient",
    )(units, ids, lanes, right, scale.reshape(cols, 1))


def update_slots(params, moment, second, stacks, places, columns, clip_factor):
    count = len(places)
    _, rows, cut = stacks[0].shape
    width = count * cut
    tile = min(rows, max(16, 131072 // cut))

    def kernel(columns_ref, clip_ref, p_ref, m_ref, v_ref, *refs):
        new_p_ref, new_m_ref, new_v_ref, grad = refs[-4:]
        c, i = pl.program_id(0), pl.program_id(1)
        start = pl.multiple_of(i * tile, tile)
        for k, (stack, place) in enumerate(places):

            @pl.when(c == k)
            def _():
                grad[...] = refs[stack][place, pl.ds(start, tile), :].astype(jnp.float32)

        new = adamw_update(p_ref[...], m_ref[...], v_ref[...], grad[...], clip_ref[0, 0])
        new_p_ref[...], new_m_ref[...], new_v_ref[...] = new

    block = pl.BlockSpec((tile, cut), lambda c, i, columns_ref: (i, columns_ref[c]))
    shape = jax.ShapeDtypeStruct((rows, width), jnp.float32)
    new = pl.pallas_call(
        kernel,
        grid_spec=pltpu.PrefetchScalarGridSpec(
            num_scalar_prefetch=1,
            grid=(count, rows // tile),
            in_specs=[pl.BlockSpec(memory_space=pltpu.SMEM)] + [block] * 3 + [whole(stack) for stack in stacks],
            out_specs=[block] * 3,
            scratch_shapes=[pltpu.VMEM((tile, cut), jnp.float32)],
        ),
        out_shape=[shape] * 3,
        compiler_params=ROOM,
        cost_estimate=cost(20 * rows * width, 26 * rows * width),
        name="update",
    )(columns, clip_factor.reshape(1, 1), *[a.reshape(rows, width) for a in (params, moment, second)], *stacks)
    return [a.reshape(params.shape) for a in new]


def join(back, scale, team):
    _, rows, cut = back.shape
    tile = min(rows, 32)

    def kernel(back_ref, scale_ref, out_ref):
        for j in range(team):
            total = back_ref[j].astype(jnp.float32) + back_ref[team + j].astype(jnp.float32)
            out_ref[:, j * cut : (j + 1) * cut] = (scale_ref[...] * total).astype(out_ref.dtype)

    return pl.pallas_call(
        kernel,
        grid=(rows // tile,),
        in_specs=[
            pl.BlockSpec((2 * team, tile, cut), lambda i: (0, i, 0)),
            pl.BlockSpec((tile, 1), lambda i: (i, 0)),
        ],
        out_specs=pl.BlockSpec((tile, team * cut), lambda i: (i, 0)),
        out_shape=jax.ShapeDtypeStruct((rows, team * cut), back.dtype),
        compiler_params=ROOM,
        cost_estimate=cost(3 * rows * team * cut, 6 * rows * team * cut),
        name="join",
    )(back, scale)


def on_device(
    acts,
    grad_out,
    row_adapter,
    ranks,
    owner_map,
    down_slots,
    up_slots,
    down_first,
    down_second,
    up_first,
    up_second,
):
    rows, width = acts.shape
    out_width = grad_out.shape[1]
    devices = lax.axis_size("dp")
    own, depth = down_slots.shape[0], down_slots.shape[1]
    slots = owner_map.shape[0]
    halves = 2
    team = devices // halves
    cut = width // team
    out_cut = out_width // team
    half_slots = own * team
    all_rows = devices * rows
    span = own * depth
    me = lax.axis_index("dp")
    seat = me % team
    f32, bf16 = jnp.float32, jnp.bfloat16

    unit_labels = jnp.arange(slots, dtype=jnp.int32)
    adapter_labels = jnp.arange(ranks.shape[0], dtype=jnp.int32)

    def describe(first_slot, count):
        here = first_slot + jnp.arange(count, dtype=jnp.int32)
        unit = jnp.sum(jnp.where(owner_map[None, :] == here[:, None], unit_labels[None, :], 0), axis=1)
        rank = jnp.sum(
            jnp.where(adapter_labels[None, :] == (unit // 2)[:, None], ranks[None, :], 0), axis=1
        )
        return unit, rank

    own_unit, own_rank = describe(me * own, own)
    keep = (own_unit % 2)[:, None] * depth + jnp.arange(depth, dtype=jnp.int32)[None, :] < own_rank[:, None]
    keep = keep.reshape(span, 1)
    down_flat = down_slots.reshape(span, width)
    up16 = jnp.where(keep, up_slots.reshape(span, out_width), 0.0).astype(bf16)

    def sliced(array, pieces):
        return array.reshape(array.shape[0], pieces, -1).transpose(1, 0, 2)

    def to_all(array):
        return lax.all_to_all(array, "dp", split_axis=0, concat_axis=0, tiled=True)

    core = seat % 2
    order = list(range(0, team, 2)) + list(range(1, team, 2))
    peers = [seat ^ b for b in order]

    def to_team(array):
        groups = [[h * team + j for j in range(team)] for h in range(halves)]
        return lax.all_to_all(array, "dp", split_axis=0, concat_axis=0, axis_index_groups=groups, tiled=True)

    def send(array, apart):
        return lax.ppermute(array, "dp", [(i, i ^ apart) for i in range(devices)])

    def swap(blocks, beside, packed=False):
        count = team // 2
        got, beside = lax.optimization_barrier((send(jnp.stack(blocks[count:]), 1), beside))
        pairs = [jnp.stack([blocks[k], got[k]]) for k in range(1, count)]
        if packed:
            pairs, beside = lax.optimization_barrier((pairs, beside))
        return beside, [blocks[0][None], got] + [send(pair, b) for pair, b in zip(pairs, order[1:])]

    def swap_back(parts):
        count = team // 2
        pairs = [send(parts[2 * k : 2 * k + 2], 2 * k) for k in range(1, count)]
        got = send(jnp.stack([parts[1]] + [pair[1] for pair in pairs]), 1)
        return [parts[:1]] + pairs + [got]

    places = [(0, 0)] + [(k + 1, 0) for k in range(1, team // 2)]
    places = places + [(1, 0)] + [(k + 1, 1) for k in range(1, team // 2)]

    def chip_sum(part):
        return part + send(part, 1)

    def team_sum(chip, beside):
        half = chip.shape[1] // 2
        mine = lax.dynamic_slice_in_dim(chip, core * half, half, axis=1)
        step = 2
        while step < team:
            other, beside = lax.optimization_barrier((send(mine.astype(bf16), step), beside))
            mine = mine + other.astype(f32)
            step *= 2
        mine = mine.astype(bf16)
        other = send(mine, 1)
        even = core == 0
        both = [jnp.where(even, mine, other), jnp.where(even, other, mine)]
        return jnp.concatenate(both, axis=1).astype(f32), beside

    def sum_over(array, steps):
        for step in steps:
            array = array + send(array, step)
        return array

    def columns_of(array, peer, size):
        return lax.dynamic_slice_in_dim(array, peer * size, size, axis=1)

    id_rows = -(-rows // out_cut)
    id_block = jnp.pad(row_adapter[:, 0], (0, id_rows * out_cut - rows)).astype(bf16)
    id_block = jnp.pad(id_block.reshape(id_rows, out_cut), ((0, -id_rows % 16), (0, 0)))
    tall = rows + id_block.shape[0]
    g_mine = jnp.concatenate([grad_out, jnp.tile(id_block, (1, team))], axis=0)
    g_other = lax.ppermute(g_mine, "dp", [(i, (i + team) % devices) for i in range(devices)])
    g_and_b = jnp.concatenate([g_mine, g_other, up16], axis=0)
    _, stacks = swap([columns_of(g_and_b, peer, out_cut) for peer in peers], ())
    acts_send = jnp.tile(sliced(acts, team), (halves, 1, 1))
    acts_send, early = lax.optimization_barrier((acts_send, stacks[:3]))
    stacks = early + stacks[3:]
    x_cut = to_all(acts_send).reshape(all_rows, cut)
    blocks = [stacks[stack][place] for stack, place in places]
    mine = jnp.zeros((team, tall, out_cut), bf16)
    theirs = mine
    for peer, block in zip(peers, blocks):
        mine = lax.dynamic_update_slice_in_dim(mine, block[None, :tall], peer, axis=0)
        theirs = lax.dynamic_update_slice_in_dim(theirs, block[None, tall : 2 * tall], peer, axis=0)
    b_cut = jnp.stack([block[2 * tall :] for block in blocks])
    lower = me < team
    g_got = jnp.concatenate([jnp.where(lower, mine, theirs), jnp.where(lower, theirs, mine)], axis=0)
    g_got = g_got.reshape(devices, tall, out_cut)
    g_cut = g_got[:, :rows].reshape(all_rows, out_cut)
    ids = g_got[:, rows : rows + id_rows].reshape(devices, -1)[:, :rows].reshape(1, all_rows)
    ids = ids.astype(f32).astype(jnp.int32)

    half_unit, half_rank = describe(me // team * half_slots, half_slots)
    seats = jnp.stack(peers)
    units = jnp.take(half_unit.reshape(team, own), seats, axis=0).reshape(-1)
    unit_rank = jnp.take(half_rank.reshape(team, own), seats, axis=0).reshape(-1)
    col_scale = adapter_alpha_value / jnp.repeat(unit_rank, depth).astype(f32)
    pair_seats = jnp.arange(team, dtype=jnp.int32) ^ seat
    pair_units = jnp.take(half_unit.reshape(team, own), pair_seats, axis=0).reshape(-1)
    pair_rank = jnp.take(half_rank.reshape(team, own), pair_seats, axis=0).reshape(-1)
    pair_scale = adapter_alpha_value / jnp.repeat(pair_rank, depth).astype(f32)
    half_scale = adapter_alpha_value / jnp.repeat(half_rank, depth).astype(f32)

    alone = [(0, k) for k in range(team)]
    low_chip = chip_sum(narrow(units, ids, g_cut, [b_cut], alone, depth))
    low_chip, down_late = lax.optimization_barrier((low_chip, down_flat))
    a_blocks = [jnp.where(keep, columns_of(down_late, peer, cut), 0.0).astype(bf16) for peer in peers]
    low_chip, a_stacks = swap(a_blocks, low_chip)
    low, _ = team_sum(low_chip, ids)
    down_parts, down_squares = gradient(pair_units, ids, low, x_cut, pair_scale, team, depth)
    down_stacks = swap_back(down_parts)
    down_places = [(k, 0) for k in range(team // 2)] + [(team // 2, k) for k in range(team // 2)]
    x_late, a_stacks, _ = lax.optimization_barrier((x_cut, a_stacks, down_parts))
    hidden_part = narrow(units, ids, x_late, a_stacks, places, depth)
    hidden_chip, a_stacks = lax.optimization_barrier((chip_sum(hidden_part), a_stacks))
    piece = pieces_of(units, ids, low, a_stacks, places, depth)
    hidden, piece = team_sum(hidden_chip, piece)
    up_parts, up_squares = gradient(half_unit, ids, hidden, g_cut, half_scale, team, depth)
    up_home = to_team(up_parts)
    far_steps = [2**k for k in range(2, devices.bit_length() - 1)][::-1]
    squares = sum_over(jnp.sum(down_squares) + jnp.sum(up_squares), far_steps)
    piece, squares, down_stacks, up_home = lax.optimization_barrier((piece, squares, down_stacks, up_home))
    squares = sum_over(squares, [1, 2])
    clip_factor = jnp.minimum(1.0, clip_limit / (jnp.sqrt(squares) + norm_eps))
    back = to_all(piece.reshape(devices, rows, cut))
    columns = jnp.stack(peers)
    down_new = update_slots(down_slots, down_first, down_second, down_stacks, down_places, columns, clip_factor)
    up_grad = up_home.transpose(1, 0, 2).reshape(own, depth, out_width).astype(f32)
    up_new = adamw_update(up_slots, up_first, up_second, up_grad, clip_factor)

    row_rank = jnp.sum(jnp.where(row_adapter == adapter_labels[None, :], ranks[None, :], 0), axis=1)
    input_grad = join(back, (adapter_alpha_value / row_rank.astype(f32))[:, None], team)
    return (input_grad, down_new[0], up_new[0], down_new[1], down_new[2], up_new[1], up_new[2])


def solution(mesh):
    two = P(("groups", "dp"), None)
    three = P(("groups", "dp"), None, None)
    return jax.shard_map(
        on_device,
        mesh=mesh,
        in_specs=(two, two, two, P(), P(), three, three, three, three, three, three),
        out_specs=(two, three, three, three, three, three, three),
        check_vma=False,
    )
```

```python
import jax
import jax.numpy as jnp
from jax import lax
from jax.experimental import pallas as pl
from jax.experimental.pallas import tpu as pltpu
from jax.sharding import PartitionSpec as P

adapter_alpha_value = 16.0
clip_limit = 1.0
norm_eps = 1e-06
beta_one = 0.9
beta_two = 0.999
bias_one = 0.9999734386011124
bias_two = 0.0952078528862904
learn_rate = 0.0002
decay_rate = 0.01
adam_eps = 1e-08


def adamw_update(params, moment, second, gradient, clip_factor):
    clipped = clip_factor * gradient
    moment = beta_one * moment + (1.0 - beta_one) * clipped
    second = beta_two * second + (1.0 - beta_two) * clipped * clipped
    params = params - learn_rate * (
        moment / bias_one / (jnp.sqrt(second / bias_two) + adam_eps) + decay_rate * params
    )
    return (params, moment, second)


ROOM = pltpu.CompilerParams(vmem_limit_bytes=28 * 1024 * 1024)
NT = (((1,), (1,)), ((), ()))
TN = (((0,), (0,)), ((), ()))


def whole(array):
    return pl.BlockSpec(array.shape, lambda *_: (0,) * array.ndim)


def cost(flops, size):
    return pl.CostEstimate(flops=flops // 4096, bytes_accessed=size // 4096, transcendentals=0)


def narrow(units, ids, left, stacks, places, depth):
    rows, span = left.shape
    size = stacks[0].shape[1]
    tile = min(rows, 512)

    def kernel(units_ref, ids_ref, left_ref, *refs):
        out_ref = refs[-1]
        twice = 2 * ids_ref[...]
        first = jnp.zeros((depth, tile), jnp.float32)
        second = first
        for c, (stack, place) in enumerate(places):
            product = lax.dot_general(refs[stack][place], left_ref[...], NT, preferred_element_type=jnp.float32)
            for k in range(size // depth):
                unit = units_ref[c * (size // depth) + k]
                lanes = product[k * depth : (k + 1) * depth]
                first = first + jnp.where(twice == unit, lanes, 0.0)
                second = second + jnp.where(twice + 1 == unit, lanes, 0.0)
        out_ref[:depth, :] = first
        out_ref[depth:, :] = second

    return pl.pallas_call(
        kernel,
        grid_spec=pltpu.PrefetchScalarGridSpec(
            num_scalar_prefetch=1,
            grid=(rows // tile,),
            in_specs=[
                pl.BlockSpec((1, tile), lambda i, _: (0, i)),
                pl.BlockSpec((tile, span), lambda i, _: (i, 0)),
            ]
            + [whole(stack) for stack in stacks],
            out_specs=pl.BlockSpec((2 * depth, tile), lambda i, _: (0, i)),
        ),
        out_shape=jax.ShapeDtypeStruct((2 * depth, rows), jnp.float32),
        compiler_params=ROOM,
        cost_estimate=cost(2 * rows * size * len(places) * span, 2 * rows * span),
        name="narrow",
    )(units, ids, left, *stacks)


def spread(unit, twice, lanes, depth):
    second = jnp.where(twice + 1 == unit, lanes[depth:], 0.0)
    return jnp.where(twice == unit, lanes[:depth], second).astype(jnp.bfloat16)


def pieces_of(units, ids, lanes, stacks, places, depth):
    rows = lanes.shape[1]
    _, size, span = stacks[0].shape
    tile = min(rows, 512)

    def kernel(units_ref, ids_ref, lanes_ref, *refs):
        out_ref, wide = refs[-2:]
        twice = 2 * ids_ref[...]
        total = jnp.zeros((tile, span), jnp.float32)
        for c, (stack, place) in enumerate(places):
            for k in range(size // depth):
                unit = units_ref[c * (size // depth) + k]
                wide[c, k * depth : (k + 1) * depth, :] = spread(unit, twice, lanes_ref[...], depth)
            total = total + lax.dot_general(
                wide[c], refs[stack][place], TN, preferred_element_type=jnp.float32
            )
        out_ref[...] = total.astype(out_ref.dtype)

    return pl.pallas_call(
        kernel,
        grid_spec=pltpu.PrefetchScalarGridSpec(
            num_scalar_prefetch=1,
            grid=(rows // tile,),
            in_specs=[
                pl.BlockSpec((1, tile), lambda i, _: (0, i)),
                pl.BlockSpec((2 * depth, tile), lambda i, _: (0, i)),
            ]
            + [whole(stack) for stack in stacks],
            out_specs=pl.BlockSpec((tile, span), lambda i, _: (i, 0)),
            scratch_shapes=[pltpu.VMEM((len(places), size, tile), jnp.bfloat16)],
        ),
        out_shape=jax.ShapeDtypeStruct((rows, span), jnp.bfloat16),
        compiler_params=ROOM,
        cost_estimate=cost(2 * rows * size * len(places) * span, 2 * rows * span),
        name="pieces",
    )(units, ids, lanes, *stacks)


def gradient(units, ids, lanes, right, scale, parts, depth):
    rows, span = right.shape
    cols = scale.shape[0] * depth
    size = cols // parts

    def kernel(units_ref, scale_ref, ids_ref, lanes_ref, right_ref, out_ref, square_ref, wide):
        b = pl.program_id(0)
        twice = 2 * ids_ref[...]
        for u in range(size // depth):
            wide[u * depth : (u + 1) * depth, :] = spread(
                units_ref[b * (size // depth) + u], twice, lanes_ref[...], depth
            )
        total = jnp.dot(wide[...], right_ref[...], preferred_element_type=jnp.float32)

        @pl.when(b == 0)
        def _():
            square_ref[...] = jnp.zeros_like(square_ref)

        for u in range(size // depth):
            part = slice(u * depth, (u + 1) * depth)
            grad = scale_ref[b * (size // depth) + u] * total[part]
            out_ref[0, part, :] = grad.astype(out_ref.dtype)
            square_ref[...] += jnp.sum(grad * grad, axis=0, keepdims=True)

    return pl.pallas_call(
        kernel,
        grid_spec=pltpu.PrefetchScalarGridSpec(
            num_scalar_prefetch=2,
            grid=(parts,),
            in_specs=[
                whole(ids),
                whole(lanes),
                whole(right),
            ],
            out_specs=[
                pl.BlockSpec((1, size, span), lambda i, *_: (i, 0, 0)),
                pl.BlockSpec((1, span), lambda i, *_: (0, 0)),
            ],
            scratch_shapes=[pltpu.VMEM((size, rows), jnp.bfloat16)],
        ),
        out_shape=[
            jax.ShapeDtypeStruct((parts, size, span), jnp.bfloat16),
            jax.ShapeDtypeStruct((1, span), jnp.float32),
        ],
        compiler_params=ROOM,
        cost_estimate=cost(2 * rows * cols * span, 2 * (rows + cols) * span),
        name="gradient",
    )(units, scale, ids, lanes, right)


def update_slots(params, moment, second, stacks, places, columns, clip_factor):
    count = len(places)
    _, rows, cut = stacks[0].shape
    width = count * cut
    tile = min(rows, max(16, 131072 // cut))

    def kernel(columns_ref, clip_ref, p_ref, m_ref, v_ref, *refs):
        new_p_ref, new_m_ref, new_v_ref, grad = refs[-4:]
        c, i = pl.program_id(0), pl.program_id(1)
        start = pl.multiple_of(i * tile, tile)
        for k, (stack, place) in enumerate(places):

            @pl.when(c == k)
            def _():
                grad[...] = refs[stack][place, pl.ds(start, tile), :].astype(jnp.float32)

        new = adamw_update(p_ref[...], m_ref[...], v_ref[...], grad[...], clip_ref[0, 0])
        new_p_ref[...], new_m_ref[...], new_v_ref[...] = new

    block = pl.BlockSpec((tile, cut), lambda c, i, columns_ref: (i, columns_ref[c]))
    shape = jax.ShapeDtypeStruct((rows, width), jnp.float32)
    new = pl.pallas_call(
        kernel,
        grid_spec=pltpu.PrefetchScalarGridSpec(
            num_scalar_prefetch=1,
            grid=(count, rows // tile),
            in_specs=[pl.BlockSpec(memory_space=pltpu.SMEM)] + [block] * 3 + [whole(stack) for stack in stacks],
            out_specs=[block] * 3,
            scratch_shapes=[pltpu.VMEM((tile, cut), jnp.float32)],
        ),
        out_shape=[shape] * 3,
        compiler_params=ROOM,
        cost_estimate=cost(20 * rows * width, 26 * rows * width),
        name="update",
    )(columns, clip_factor.reshape(1, 1), *[a.reshape(rows, width) for a in (params, moment, second)], *stacks)
    return [a.reshape(params.shape) for a in new]


def join(back, scale, team):
    _, rows, cut = back.shape
    tile = min(rows, 32)

    def kernel(back_ref, scale_ref, out_ref):
        for j in range(team):
            total = back_ref[j].astype(jnp.float32) + back_ref[team + j].astype(jnp.float32)
            out_ref[:, j * cut : (j + 1) * cut] = (scale_ref[...] * total).astype(out_ref.dtype)

    return pl.pallas_call(
        kernel,
        grid=(rows // tile,),
        in_specs=[
            pl.BlockSpec((2 * team, tile, cut), lambda i: (0, i, 0)),
            pl.BlockSpec((tile, 1), lambda i: (i, 0)),
        ],
        out_specs=pl.BlockSpec((tile, team * cut), lambda i: (i, 0)),
        out_shape=jax.ShapeDtypeStruct((rows, team * cut), back.dtype),
        compiler_params=ROOM,
        cost_estimate=cost(3 * rows * team * cut, 6 * rows * team * cut),
        name="join",
    )(back, scale)


def on_device(
    acts,
    grad_out,
    row_adapter,
    ranks,
    owner_map,
    down_slots,
    up_slots,
    down_first,
    down_second,
    up_first,
    up_second,
):
    rows, width = acts.shape
    out_width = grad_out.shape[1]
    devices = lax.axis_size("dp")
    own, depth = down_slots.shape[0], down_slots.shape[1]
    slots = owner_map.shape[0]
    halves = 2
    team = devices // halves
    cut = width // team
    out_cut = out_width // team
    half_slots = own * team
    all_rows = devices * rows
    span = own * depth
    me = lax.axis_index("dp")
    seat = me % team
    f32, bf16 = jnp.float32, jnp.bfloat16

    unit_labels = jnp.arange(slots, dtype=jnp.int32)
    adapter_labels = jnp.arange(ranks.shape[0], dtype=jnp.int32)

    def describe(first_slot, count):
        here = first_slot + jnp.arange(count, dtype=jnp.int32)
        unit = jnp.sum(jnp.where(owner_map[None, :] == here[:, None], unit_labels[None, :], 0), axis=1)
        rank = jnp.sum(
            jnp.where(adapter_labels[None, :] == (unit // 2)[:, None], ranks[None, :], 0), axis=1
        )
        return unit, rank

    own_unit, own_rank = describe(me * own, own)
    keep = (own_unit % 2)[:, None] * depth + jnp.arange(depth, dtype=jnp.int32)[None, :] < own_rank[:, None]
    keep = keep.reshape(span, 1)
    down_flat = down_slots.reshape(span, width)
    up16 = jnp.where(keep, up_slots.reshape(span, out_width), 0.0).astype(bf16)

    def sliced(array, pieces):
        return array.reshape(array.shape[0], pieces, -1).transpose(1, 0, 2)

    def to_all(array):
        return lax.all_to_all(array, "dp", split_axis=0, concat_axis=0, tiled=True)

    core = seat % 2
    order = list(range(0, team, 2)) + list(range(1, team, 2))
    peers = [seat ^ b for b in order]

    def to_team(array):
        groups = [[h * team + j for j in range(team)] for h in range(halves)]
        return lax.all_to_all(array, "dp", split_axis=0, concat_axis=0, axis_index_groups=groups, tiled=True)

    def send(array, apart):
        return lax.ppermute(array, "dp", [(i, i ^ apart) for i in range(devices)])

    def swap(blocks, beside, packed=False):
        count = team // 2
        got, beside = lax.optimization_barrier((send(jnp.stack(blocks[count:]), 1), beside))
        pairs = [jnp.stack([blocks[k], got[k]]) for k in range(1, count)]
        if packed:
            pairs, beside = lax.optimization_barrier((pairs, beside))
        return beside, [blocks[0][None], got] + [send(pair, b) for pair, b in zip(pairs, order[1:])]

    def swap_back(parts):
        count = team // 2
        pairs = [send(parts[2 * k : 2 * k + 2], 2 * k) for k in range(1, count)]
        got = send(jnp.stack([parts[1]] + [pair[1] for pair in pairs]), 1)
        return [parts[:1]] + pairs + [got]

    places = [(0, 0)] + [(k + 1, 0) for k in range(1, team // 2)]
    places = places + [(1, 0)] + [(k + 1, 1) for k in range(1, team // 2)]

    def chip_sum(part):
        return part + send(part, 1)

    def team_sum(chip, beside):
        half = chip.shape[1] // 2
        mine = lax.dynamic_slice_in_dim(chip, core * half, half, axis=1)
        step = 2
        while step < team:
            other, beside = lax.optimization_barrier((send(mine.astype(bf16), step), beside))
            mine = mine + other.astype(f32)
            step *= 2
        mine = mine.astype(bf16)
        other = send(mine, 1)
        even = core == 0
        both = [jnp.where(even, mine, other), jnp.where(even, other, mine)]
        return jnp.concatenate(both, axis=1).astype(f32), beside

    def sum_over(array, steps):
        for step in steps:
            array = array + send(array, step)
        return array

    def columns_of(array, peer, size):
        return lax.dynamic_slice_in_dim(array, peer * size, size, axis=1)

    id_rows = -(-rows // out_cut)
    id_block = jnp.pad(row_adapter[:, 0], (0, id_rows * out_cut - rows)).astype(bf16)
    id_block = jnp.pad(id_block.reshape(id_rows, out_cut), ((0, -id_rows % 16), (0, 0)))
    tall = rows + id_block.shape[0]
    g_mine = jnp.concatenate([grad_out, jnp.tile(id_block, (1, team))], axis=0)
    g_other = lax.ppermute(g_mine, "dp", [(i, (i + team) % devices) for i in range(devices)])
    acts_send = jnp.tile(sliced(acts, team), (halves, 1, 1))
    g_other, acts_send = lax.optimization_barrier((g_other, acts_send))
    g_and_b = jnp.concatenate([g_mine, g_other, up16], axis=0)
    acts_send, stacks = swap([columns_of(g_and_b, peer, out_cut) for peer in peers], acts_send, True)
    x_cut = to_all(acts_send).reshape(all_rows, cut)
    blocks = [stacks[stack][place] for stack, place in places]
    mine = jnp.zeros((team, tall, out_cut), bf16)
    theirs = mine
    for peer, block in zip(peers, blocks):
        mine = lax.dynamic_update_slice_in_dim(mine, block[None, :tall], peer, axis=0)
        theirs = lax.dynamic_update_slice_in_dim(theirs, block[None, tall : 2 * tall], peer, axis=0)
    b_cut = jnp.stack([block[2 * tall :] for block in blocks])
    lower = me < team
    g_got = jnp.concatenate([jnp.where(lower, mine, theirs), jnp.where(lower, theirs, mine)], axis=0)
    g_got = g_got.reshape(devices, tall, out_cut)
    g_cut = g_got[:, :rows].reshape(all_rows, out_cut)
    ids = g_got[:, rows : rows + id_rows].reshape(devices, -1)[:, :rows].reshape(1, all_rows)
    ids = ids.astype(f32).astype(jnp.int32)

    half_unit, half_rank = describe(me // team * half_slots, half_slots)
    seats = jnp.stack(peers)
    units = jnp.take(half_unit.reshape(team, own), seats, axis=0).reshape(-1)
    unit_rank = jnp.take(half_rank.reshape(team, own), seats, axis=0).reshape(-1)
    col_scale = adapter_alpha_value / jnp.repeat(unit_rank, depth).astype(f32)
    pair_seats = jnp.arange(team, dtype=jnp.int32) ^ seat
    pair_units = jnp.take(half_unit.reshape(team, own), pair_seats, axis=0).reshape(-1)
    pair_rank = jnp.take(half_rank.reshape(team, own), pair_seats, axis=0).reshape(-1)
    pair_scale = adapter_alpha_value / pair_rank.astype(f32)
    half_scale = adapter_alpha_value / half_rank.astype(f32)

    alone = [(0, k) for k in range(team)]
    low_chip = chip_sum(narrow(units, ids, g_cut, [b_cut], alone, depth))
    low_chip, down_late = lax.optimization_barrier((low_chip, down_flat))
    a_blocks = [jnp.where(keep, columns_of(down_late, peer, cut), 0.0).astype(bf16) for peer in peers]
    low_chip, a_stacks = swap(a_blocks, low_chip)
    low, _ = team_sum(low_chip, ids)
    down_parts, down_squares = gradient(pair_units, ids, low, x_cut, pair_scale, team, depth)
    down_stacks = swap_back(down_parts)
    down_places = [(k, 0) for k in range(team // 2)] + [(team // 2, k) for k in range(team // 2)]
    x_late, a_stacks, _ = lax.optimization_barrier((x_cut, a_stacks, down_parts))
    hidden_part = narrow(units, ids, x_late, a_stacks, places, depth)
    hidden_chip, a_stacks = lax.optimization_barrier((chip_sum(hidden_part), a_stacks))
    piece = pieces_of(units, ids, low, a_stacks, places, depth)
    hidden, piece = team_sum(hidden_chip, piece)
    up_parts, up_squares = gradient(half_unit, ids, hidden, g_cut, half_scale, team, depth)
    up_home = to_team(up_parts)
    far_steps = [2**k for k in range(2, devices.bit_length() - 1)][::-1]
    squares = sum_over(jnp.sum(jnp.concatenate([down_squares, up_squares], axis=1)), far_steps)
    piece, squares, down_stacks, up_home = lax.optimization_barrier((piece, squares, down_stacks, up_home))
    squares = sum_over(squares, [1, 2])
    clip_factor = jnp.minimum(1.0, clip_limit / (jnp.sqrt(squares) + norm_eps))
    back = to_all(piece.reshape(devices, rows, cut))
    columns = jnp.stack(peers)
    down_new = update_slots(down_slots, down_first, down_second, down_stacks, down_places, columns, clip_factor)
    up_grad = up_home.transpose(1, 0, 2).reshape(own, depth, out_width).astype(f32)
    up_new = adamw_update(up_slots, up_first, up_second, up_grad, clip_factor)

    row_rank = jnp.sum(jnp.where(row_adapter == adapter_labels[None, :], ranks[None, :], 0), axis=1)
    input_grad = join(back, (adapter_alpha_value / row_rank.astype(f32))[:, None], team)
    return (input_grad, down_new[0], up_new[0], down_new[1], down_new[2], up_new[1], up_new[2])


def solution(mesh):
    two = P(("groups", "dp"), None)
    three = P(("groups", "dp"), None, None)
    return jax.shard_map(
        on_device,
        mesh=mesh,
        in_specs=(two, two, two, P(), P(), three, three, three, three, three, three),
        out_specs=(two, three, three, three, three, three, three),
        check_vma=False,
    )
```

```python
import jax
import jax.numpy as jnp
from jax import lax
from jax.experimental import pallas as pl
from jax.experimental.pallas import tpu as pltpu
from jax.sharding import PartitionSpec as P

adapter_alpha_value = 16.0
clip_limit = 1.0
norm_eps = 1e-06
beta_one = 0.9
beta_two = 0.999
bias_one = 0.9999734386011124
bias_two = 0.0952078528862904
learn_rate = 0.0002
decay_rate = 0.01
adam_eps = 1e-08


def adamw_update(params, moment, second, gradient, clip_factor):
    clipped = clip_factor * gradient
    moment = beta_one * moment + (1.0 - beta_one) * clipped
    second = beta_two * second + (1.0 - beta_two) * clipped * clipped
    params = params - learn_rate * (
        moment / bias_one / (jnp.sqrt(second / bias_two) + adam_eps) + decay_rate * params
    )
    return (params, moment, second)


ROOM = pltpu.CompilerParams(vmem_limit_bytes=28 * 1024 * 1024)
NT = (((1,), (1,)), ((), ()))
TN = (((0,), (0,)), ((), ()))


def whole(array):
    return pl.BlockSpec(array.shape, lambda *_: (0,) * array.ndim)


def cost(flops, size):
    return pl.CostEstimate(flops=flops // 4096, bytes_accessed=size // 4096, transcendentals=0)


def narrow(units, ids, left, stacks, places, depth):
    rows, span = left.shape
    size = stacks[0].shape[1]
    tile = min(rows, 512)

    def kernel(units_ref, ids_ref, left_ref, *refs):
        out_ref = refs[-1]
        twice = 2 * ids_ref[...]
        first = jnp.zeros((depth, tile), jnp.float32)
        second = first
        for c, (stack, place) in enumerate(places):
            product = lax.dot_general(refs[stack][place], left_ref[...], NT, preferred_element_type=jnp.float32)
            for k in range(size // depth):
                unit = units_ref[c * (size // depth) + k]
                lanes = product[k * depth : (k + 1) * depth]
                first = first + jnp.where(twice == unit, lanes, 0.0)
                second = second + jnp.where(twice + 1 == unit, lanes, 0.0)
        out_ref[:depth, :] = first
        out_ref[depth:, :] = second

    return pl.pallas_call(
        kernel,
        grid_spec=pltpu.PrefetchScalarGridSpec(
            num_scalar_prefetch=1,
            grid=(rows // tile,),
            in_specs=[
                pl.BlockSpec((1, tile), lambda i, _: (0, i)),
                pl.BlockSpec((tile, span), lambda i, _: (i, 0)),
            ]
            + [whole(stack) for stack in stacks],
            out_specs=pl.BlockSpec((2 * depth, tile), lambda i, _: (0, i)),
        ),
        out_shape=jax.ShapeDtypeStruct((2 * depth, rows), jnp.float32),
        compiler_params=ROOM,
        cost_estimate=cost(2 * rows * size * len(places) * span, 2 * rows * span),
        name="narrow",
    )(units, ids, left, *stacks)


def spread(unit, twice, lanes, depth):
    second = jnp.where(twice + 1 == unit, lanes[depth:], 0.0)
    return jnp.where(twice == unit, lanes[:depth], second).astype(jnp.bfloat16)


def pieces_of(units, ids, lanes, stacks, places, depth):
    rows = lanes.shape[1]
    _, size, span = stacks[0].shape
    tile = min(rows, 512)

    def kernel(units_ref, ids_ref, lanes_ref, *refs):
        out_ref, wide = refs[-2:]
        twice = 2 * ids_ref[...]
        total = jnp.zeros((tile, span), jnp.float32)
        for c, (stack, place) in enumerate(places):
            for k in range(size // depth):
                unit = units_ref[c * (size // depth) + k]
                wide[c, k * depth : (k + 1) * depth, :] = spread(unit, twice, lanes_ref[...], depth)
            total = total + lax.dot_general(
                wide[c], refs[stack][place], TN, preferred_element_type=jnp.float32
            )
        out_ref[...] = total.astype(out_ref.dtype)

    return pl.pallas_call(
        kernel,
        grid_spec=pltpu.PrefetchScalarGridSpec(
            num_scalar_prefetch=1,
            grid=(rows // tile,),
            in_specs=[
                pl.BlockSpec((1, tile), lambda i, _: (0, i)),
                pl.BlockSpec((2 * depth, tile), lambda i, _: (0, i)),
            ]
            + [whole(stack) for stack in stacks],
            out_specs=pl.BlockSpec((tile, span), lambda i, _: (i, 0)),
            scratch_shapes=[pltpu.VMEM((len(places), size, tile), jnp.bfloat16)],
        ),
        out_shape=jax.ShapeDtypeStruct((rows, span), jnp.bfloat16),
        compiler_params=ROOM,
        cost_estimate=cost(2 * rows * size * len(places) * span, 2 * rows * span),
        name="pieces",
    )(units, ids, lanes, *stacks)


def gradient(units, ids, lanes, right, scale, parts, depth):
    rows, span = right.shape
    cols = scale.shape[0] * depth
    size = cols // parts

    def kernel(units_ref, scale_ref, ids_ref, lanes_ref, right_ref, out_ref, square_ref, wide):
        b = pl.program_id(0)
        twice = 2 * ids_ref[...]
        for u in range(size // depth):
            wide[u * depth : (u + 1) * depth, :] = spread(
                units_ref[b * (size // depth) + u], twice, lanes_ref[...], depth
            )
        total = jnp.dot(wide[...], right_ref[...], preferred_element_type=jnp.float32)

        @pl.when(b == 0)
        def _():
            square_ref[...] = jnp.zeros_like(square_ref)

        for u in range(size // depth):
            part = slice(u * depth, (u + 1) * depth)
            grad = scale_ref[b * (size // depth) + u] * total[part]
            out_ref[0, part, :] = grad.astype(out_ref.dtype)
            square_ref[...] += jnp.sum(grad * grad, axis=0, keepdims=True)

    return pl.pallas_call(
        kernel,
        grid_spec=pltpu.PrefetchScalarGridSpec(
            num_scalar_prefetch=2,
            grid=(parts,),
            in_specs=[
                whole(ids),
                whole(lanes),
                whole(right),
            ],
            out_specs=[
                pl.BlockSpec((1, size, span), lambda i, *_: (i, 0, 0)),
                pl.BlockSpec((1, span), lambda i, *_: (0, 0)),
            ],
            scratch_shapes=[pltpu.VMEM((size, rows), jnp.bfloat16)],
        ),
        out_shape=[
            jax.ShapeDtypeStruct((parts, size, span), jnp.bfloat16),
            jax.ShapeDtypeStruct((1, span), jnp.float32),
        ],
        compiler_params=ROOM,
        cost_estimate=cost(2 * rows * cols * span, 2 * (rows + cols) * span),
        name="gradient",
    )(units, scale, ids, lanes, right)


def update_slots(params, moment, second, stacks, places, columns, clip_factor):
    count = len(places)
    _, rows, cut = stacks[0].shape
    width = count * cut
    tile = min(rows, max(16, 131072 // cut))

    def kernel(columns_ref, clip_ref, p_ref, m_ref, v_ref, *refs):
        new_p_ref, new_m_ref, new_v_ref, grad = refs[-4:]
        c, i = pl.program_id(0), pl.program_id(1)
        start = pl.multiple_of(i * tile, tile)
        for k, (stack, place) in enumerate(places):

            @pl.when(c == k)
            def _():
                grad[...] = refs[stack][place, pl.ds(start, tile), :].astype(jnp.float32)

        new = adamw_update(p_ref[...], m_ref[...], v_ref[...], grad[...], clip_ref[0, 0])
        new_p_ref[...], new_m_ref[...], new_v_ref[...] = new

    block = pl.BlockSpec((tile, cut), lambda c, i, columns_ref: (i, columns_ref[c]))
    shape = jax.ShapeDtypeStruct((rows, width), jnp.float32)
    new = pl.pallas_call(
        kernel,
        grid_spec=pltpu.PrefetchScalarGridSpec(
            num_scalar_prefetch=1,
            grid=(count, rows // tile),
            in_specs=[pl.BlockSpec(memory_space=pltpu.SMEM)] + [block] * 3 + [whole(stack) for stack in stacks],
            out_specs=[block] * 3,
            scratch_shapes=[pltpu.VMEM((tile, cut), jnp.float32)],
        ),
        out_shape=[shape] * 3,
        compiler_params=ROOM,
        cost_estimate=cost(20 * rows * width, 26 * rows * width),
        name="update",
    )(columns, clip_factor.reshape(1, 1), *[a.reshape(rows, width) for a in (params, moment, second)], *stacks)
    return [a.reshape(params.shape) for a in new]


def join(back, scale, team):
    _, rows, cut = back.shape
    tile = min(rows, 16)

    def kernel(back_ref, scale_ref, out_ref):
        for j in range(team):
            total = back_ref[j].astype(jnp.float32) + back_ref[team + j].astype(jnp.float32)
            out_ref[:, j * cut : (j + 1) * cut] = (scale_ref[...] * total).astype(out_ref.dtype)

    return pl.pallas_call(
        kernel,
        grid=(rows // tile,),
        in_specs=[
            pl.BlockSpec((2 * team, tile, cut), lambda i: (0, i, 0)),
            pl.BlockSpec((tile, 1), lambda i: (i, 0)),
        ],
        out_specs=pl.BlockSpec((tile, team * cut), lambda i: (i, 0)),
        out_shape=jax.ShapeDtypeStruct((rows, team * cut), back.dtype),
        compiler_params=ROOM,
        cost_estimate=cost(3 * rows * team * cut, 6 * rows * team * cut),
        name="join",
    )(back, scale)


def on_device(
    acts,
    grad_out,
    row_adapter,
    ranks,
    owner_map,
    down_slots,
    up_slots,
    down_first,
    down_second,
    up_first,
    up_second,
):
    rows, width = acts.shape
    out_width = grad_out.shape[1]
    devices = lax.axis_size("dp")
    own, depth = down_slots.shape[0], down_slots.shape[1]
    slots = owner_map.shape[0]
    halves = 2
    team = devices // halves
    cut = width // team
    out_cut = out_width // team
    half_slots = own * team
    all_rows = devices * rows
    span = own * depth
    me = lax.axis_index("dp")
    seat = me % team
    f32, bf16 = jnp.float32, jnp.bfloat16

    unit_labels = jnp.arange(slots, dtype=jnp.int32)
    adapter_labels = jnp.arange(ranks.shape[0], dtype=jnp.int32)

    def describe(first_slot, count):
        here = first_slot + jnp.arange(count, dtype=jnp.int32)
        unit = jnp.sum(jnp.where(owner_map[None, :] == here[:, None], unit_labels[None, :], 0), axis=1)
        rank = jnp.sum(
            jnp.where(adapter_labels[None, :] == (unit // 2)[:, None], ranks[None, :], 0), axis=1
        )
        return unit, rank

    own_unit, own_rank = describe(me * own, own)
    keep = (own_unit % 2)[:, None] * depth + jnp.arange(depth, dtype=jnp.int32)[None, :] < own_rank[:, None]
    keep = keep.reshape(span, 1)
    down_flat = down_slots.reshape(span, width)
    up16 = jnp.where(keep, up_slots.reshape(span, out_width), 0.0).astype(bf16)

    def sliced(array, pieces):
        return array.reshape(array.shape[0], pieces, -1).transpose(1, 0, 2)

    def to_all(array):
        return lax.all_to_all(array, "dp", split_axis=0, concat_axis=0, tiled=True)

    core = seat % 2
    order = list(range(0, team, 2)) + list(range(1, team, 2))
    peers = [seat ^ b for b in order]

    def to_team(array):
        groups = [[h * team + j for j in range(team)] for h in range(halves)]
        return lax.all_to_all(array, "dp", split_axis=0, concat_axis=0, axis_index_groups=groups, tiled=True)

    def send(array, apart):
        return lax.ppermute(array, "dp", [(i, i ^ apart) for i in range(devices)])

    def swap(blocks, beside, packed=False):
        count = team // 2
        got, beside = lax.optimization_barrier((send(jnp.stack(blocks[count:]), 1), beside))
        pairs = [jnp.stack([blocks[k], got[k]]) for k in range(1, count)]
        if packed:
            pairs, beside = lax.optimization_barrier((pairs, beside))
        return beside, [blocks[0][None], got] + [send(pair, b) for pair, b in zip(pairs, order[1:])]

    def swap_back(parts):
        count = team // 2
        pairs = [send(parts[2 * k : 2 * k + 2], 2 * k) for k in range(1, count)]
        got = send(jnp.stack([parts[1]] + [pair[1] for pair in pairs]), 1)
        return [parts[:1]] + pairs + [got]

    places = [(0, 0)] + [(k + 1, 0) for k in range(1, team // 2)]
    places = places + [(1, 0)] + [(k + 1, 1) for k in range(1, team // 2)]

    def chip_sum(part):
        return part + send(part, 1)

    def team_sum(chip, beside):
        half = chip.shape[1] // 2
        mine = lax.dynamic_slice_in_dim(chip, core * half, half, axis=1)
        step = 2
        while step < team:
            other, beside = lax.optimization_barrier((send(mine.astype(bf16), step), beside))
            mine = mine + other.astype(f32)
            step *= 2
        mine = mine.astype(bf16)
        other = send(mine, 1)
        even = core == 0
        both = [jnp.where(even, mine, other), jnp.where(even, other, mine)]
        return jnp.concatenate(both, axis=1).astype(f32), beside

    def sum_over(array, steps):
        for step in steps:
            array = array + send(array, step)
        return array

    def columns_of(array, peer, size):
        return lax.dynamic_slice_in_dim(array, peer * size, size, axis=1)

    id_rows = -(-rows // out_cut)
    id_block = jnp.pad(row_adapter[:, 0], (0, id_rows * out_cut - rows)).astype(bf16)
    id_block = jnp.pad(id_block.reshape(id_rows, out_cut), ((0, -id_rows % 16), (0, 0)))
    tall = rows + id_block.shape[0]
    g_mine = jnp.concatenate([grad_out, jnp.tile(id_block, (1, team))], axis=0)
    g_other = lax.ppermute(g_mine, "dp", [(i, (i + team) % devices) for i in range(devices)])
    acts_send = jnp.tile(sliced(acts, team), (halves, 1, 1))
    g_other, acts_send = lax.optimization_barrier((g_other, acts_send))
    g_and_b = jnp.concatenate([g_mine, g_other, up16], axis=0)
    acts_send, stacks = swap([columns_of(g_and_b, peer, out_cut) for peer in peers], acts_send, True)
    x_cut = to_all(acts_send).reshape(all_rows, cut)
    blocks = [stacks[stack][place] for stack, place in places]
    mine = jnp.zeros((team, tall, out_cut), bf16)
    theirs = mine
    for peer, block in zip(peers, blocks):
        mine = lax.dynamic_update_slice_in_dim(mine, block[None, :tall], peer, axis=0)
        theirs = lax.dynamic_update_slice_in_dim(theirs, block[None, tall : 2 * tall], peer, axis=0)
    b_cut = jnp.stack([block[2 * tall :] for block in blocks])
    lower = me < team
    g_got = jnp.concatenate([jnp.where(lower, mine, theirs), jnp.where(lower, theirs, mine)], axis=0)
    g_got = g_got.reshape(devices, tall, out_cut)
    g_cut = g_got[:, :rows].reshape(all_rows, out_cut)
    ids = g_got[:, rows : rows + id_rows].reshape(devices, -1)[:, :rows].reshape(1, all_rows)
    ids = ids.astype(f32).astype(jnp.int32)

    half_unit, half_rank = describe(me // team * half_slots, half_slots)
    seats = jnp.stack(peers)
    units = jnp.take(half_unit.reshape(team, own), seats, axis=0).reshape(-1)
    unit_rank = jnp.take(half_rank.reshape(team, own), seats, axis=0).reshape(-1)
    col_scale = adapter_alpha_value / jnp.repeat(unit_rank, depth).astype(f32)
    pair_seats = jnp.arange(team, dtype=jnp.int32) ^ seat
    pair_units = jnp.take(half_unit.reshape(team, own), pair_seats, axis=0).reshape(-1)
    pair_rank = jnp.take(half_rank.reshape(team, own), pair_seats, axis=0).reshape(-1)
    pair_scale = adapter_alpha_value / pair_rank.astype(f32)
    half_scale = adapter_alpha_value / half_rank.astype(f32)

    alone = [(0, k) for k in range(team)]
    low_chip = chip_sum(narrow(units, ids, g_cut, [b_cut], alone, depth))
    low_chip, down_late = lax.optimization_barrier((low_chip, down_flat))
    a_blocks = [jnp.where(keep, columns_of(down_late, peer, cut), 0.0).astype(bf16) for peer in peers]
    low_chip, a_stacks = swap(a_blocks, low_chip)
    low, _ = team_sum(low_chip, ids)
    down_parts, down_squares = gradient(pair_units, ids, low, x_cut, pair_scale, team, depth)
    down_stacks = swap_back(down_parts)
    down_places = [(k, 0) for k in range(team // 2)] + [(team // 2, k) for k in range(team // 2)]
    x_late, a_stacks, _ = lax.optimization_barrier((x_cut, a_stacks, down_parts))
    hidden_part = narrow(units, ids, x_late, a_stacks, places, depth)
    hidden_chip, a_stacks = lax.optimization_barrier((chip_sum(hidden_part), a_stacks))
    piece = pieces_of(units, ids, low, a_stacks, places, depth)
    hidden, piece = team_sum(hidden_chip, piece)
    up_parts, up_squares = gradient(half_unit, ids, hidden, g_cut, half_scale, team, depth)
    up_home = to_team(up_parts)
    far_steps = [2**k for k in range(2, devices.bit_length() - 1)][::-1]
    squares = sum_over(jnp.sum(jnp.concatenate([down_squares, up_squares], axis=1)), far_steps)
    piece, squares, down_stacks, up_home = lax.optimization_barrier((piece, squares, down_stacks, up_home))
    squares = sum_over(squares, [1, 2])
    clip_factor = jnp.minimum(1.0, clip_limit / (jnp.sqrt(squares) + norm_eps))
    back = to_all(piece.reshape(devices, rows, cut))
    columns = jnp.stack(peers)
    down_new = update_slots(down_slots, down_first, down_second, down_stacks, down_places, columns, clip_factor)
    up_grad = up_home.transpose(1, 0, 2).reshape(own, depth, out_width).astype(f32)
    up_new = adamw_update(up_slots, up_first, up_second, up_grad, clip_factor)

    row_rank = jnp.sum(jnp.where(row_adapter == adapter_labels[None, :], ranks[None, :], 0), axis=1)
    input_grad = join(back, (adapter_alpha_value / row_rank.astype(f32))[:, None], team)
    return (input_grad, down_new[0], up_new[0], down_new[1], down_new[2], up_new[1], up_new[2])


def solution(mesh):
    two = P(("groups", "dp"), None)
    three = P(("groups", "dp"), None, None)
    return jax.shard_map(
        on_device,
        mesh=mesh,
        in_specs=(two, two, two, P(), P(), three, three, three, three, three, three),
        out_specs=(two, three, three, three, three, three, three),
        check_vma=False,
    )
```
